32 devices in a mesh: sector: 4 (over y, x), win: 8 (over z, core).
Axes of the slice: x: 2, y: 2, z: 4, core: 2. Of those that a mesh axis runs over, the one named last changes fastest.
Arguments:
- observed: float32 [2, 64, 128, 128], P(None, 'sector', 'win'), may hold values from -12 to 12
- psf_bank: float32 [16, 2, 2, 16, 1024], P('sector'), may hold values from -0.03125 to 0.03125
- psf_ids: int32 [4, 8, 4], P(None, 'win'), may hold values from 0 to 15
- weight_ids: int32 [4, 8, 4], P(None, 'win'), may hold values from 0 to 15
- list_counts: int32 [4, 8], P(None, 'win'), may hold values from 1 to 4
Outputs:
- solution: float32 [2, 64, 128, 128], P(None, 'sector', 'win')
- residual: float32 [2, 64, 128, 128], P(None, 'sector', 'win')
The draws below stay inside these ranges and needn't reach their ends.
Inputs may be any that keep to these rules, and one draw needn't show every extreme that they name: `psf_ids`: row numbers of psf_bank; entries at and after a window's count are not used.
All inputs are finite; a program needn't handle non-finite values.
Results may differ from the reference program's by a relative error of at most 0.00029.
Values sent between devices are 32-bit elements; how exact they have to be, the bound alone decides.
A program may use at most 128 MiB of HBM per device.

```python
import math
import jax
import jax.numpy as jnp
import numpy as np
from jax import lax

CX = 16
CY = 16
NZ = 128
KL = 32
KD = 16
LMAX = 4
NW = 16
ITERS = 2
GX = 4
GY = 8
NX = 64
NY = 128
NPSF = 16


def draw_observed(key, part):
    first = jnp.arange(NX, dtype=jnp.float32) / max(NX - 1, 1)
    second = jnp.arange(NY, dtype=jnp.float32) / max(NY - 1, 1)
    ramp = jnp.exp(0.5 * math.log(3.0) * (first[:, None] + second[None, :]))[None, :, :, None]
    noise = jnp.clip(jax.random.normal(key, (2, NX, NY, NZ), jnp.float32), -4.0, 4.0)
    return noise * ramp


def draw_list_counts(key, part):
    key_counts, key_top, key_low = jax.random.split(key, 3)
    counts = jax.random.randint(key_counts, (GX * GY,), 1, LMAX + 1, dtype=jnp.int32)
    top_window = jax.random.randint(key_top, (), 0, GX * GY, dtype=jnp.int32)
    low_window = (top_window + 1 + jax.random.randint(key_low, (), 0, GX * GY - 1, dtype=jnp.int32)) % (GX * GY)
    counts = counts.at[top_window].set(LMAX).at[low_window].set(1)
    return counts.reshape(GX, GY)


def plant(entries, own_key, smallest, top_value):
    place = [jax.random.randint(jax.random.fold_in(own_key, axis), (), 0, length) for axis, length in enumerate(entries.shape)]
    main_axis = entries.shape.index(max(entries.shape))
    beside = place[:main_axis] + [(place[main_axis] + 1) % entries.shape[main_axis]] + place[main_axis + 1:]
    return entries.at[tuple(place)].set(smallest).at[tuple(beside)].set(top_value)


def level_of(key, extent, shards, least, top_value):
    def one(position, parts):
        draws = jax.random.uniform(jax.random.fold_in(jax.random.fold_in(key, 6), position), (parts,), jnp.float32, least / len(shards), top_value / len(shards))
        return jnp.repeat(jnp.exp(draws), extent[position] // parts).reshape((-1,) + (1,) * (len(extent) - position - 1))

    loudness = one(*shards[0])
    for cut in shards[1:]:
        loudness = loudness * one(*cut)
    return loudness


def rank_table(count, skew):
    portions = [(1 << 20) // math.isqrt(standing ** skew) + 1 for standing in range(1, count + 1)]
    deviation = 1 + sum(portions) // (1 << 30)
    return np.cumsum(np.array([max(1, weight // deviation) for weight in portions]))


def ranked(own_key, shape, count, skew):
    table = rank_table(count, skew)
    lot = jax.random.randint(jax.random.fold_in(own_key, 1), shape, 0, int(table[count - 1]))
    rank = jnp.searchsorted(jnp.asarray(table, jnp.int32), lot, side="right")
    return jax.random.permutation(jax.random.fold_in(own_key, 2), count)[rank].astype(jnp.int32)


def bell_draw(own_key, dims, width, limit, shards=(), kind=jnp.bfloat16):
    loudness = level_of(own_key, dims, shards, -0.22, 0.18) if shards else 1.0
    values = jax.random.normal(own_key, dims, jnp.float32) * width * loudness
    return jnp.minimum(jnp.maximum(values, -limit), limit).astype(kind)


def setup_inputs(seed: int = 0) -> dict:
    key_list = jax.random.split(jax.random.key(seed), 6)
    return {
        "observed": draw_observed(jax.random.fold_in(key_list[5], 71), 0),
        "psf_bank": bell_draw(key_list[1], (NPSF, 2, 2, KD, KL * KL), (2 * KL * KL * KD) ** -0.5, 0.03125, ((0, 4),), jnp.float32),
        "psf_ids": plant(ranked(key_list[2], (GX, GY, LMAX), NPSF, 2), jax.random.fold_in(key_list[2], 3), 0, NPSF - 1).astype(jnp.int32),
        "weight_ids": plant(jax.random.randint(key_list[3], (GX, GY, LMAX), 0, NW), jax.random.fold_in(key_list[3], 1), 0, NW - 1).astype(jnp.int32),
        "list_counts": draw_list_counts(jax.random.fold_in(key_list[5], 71), 0),
    }


def window_spectrum(psf_bank, psf_ids, weight_ids, list_counts, row_x, row_y):
    chosen = psf_ids[row_x, row_y]
    in_list = (jnp.arange(LMAX, dtype=jnp.int32) < list_counts[row_x, row_y]).astype(psf_bank.dtype)
    factors = in_list * (weight_ids[row_x, row_y].astype(psf_bank.dtype) + 1.0) / NW
    picked = psf_bank[chosen].reshape(LMAX, -1)
    blended = jnp.einsum('l,lm->m', factors, picked, precision=lax.Precision.HIGHEST)
    kernel = blended.reshape(2, 2, KD, KL, KL).transpose(0, 1, 3, 4, 2)
    kernel = jnp.pad(kernel, ((0, 0), (0, 0), (0, CX), (0, CY), (0, NZ)))
    kernel = jnp.roll(kernel, -(KD // 2), axis=4)
    return jnp.fft.fftn(kernel, axes=(2, 3, 4))


def apply_forward(field, psf_bank, psf_ids, weight_ids, list_counts):
    margin = KL // 2
    padded = jnp.pad(field, ((0, 0), (margin, margin), (margin, margin), (0, 0)))
    zero_index = jnp.zeros((), jnp.int32)

    def one_window(index, result):
        index = jnp.asarray(index).astype(jnp.int32)
        row_x = index // GY
        row_y = index % GY
        spectrum = window_spectrum(psf_bank, psf_ids, weight_ids, list_counts, row_x, row_y)
        start = (zero_index, row_x * CX, row_y * CY, zero_index)
        extended = lax.dynamic_slice(padded, start, (2, CX + KL, CY + KL, NZ))
        extended = jnp.pad(extended, ((0, 0), (0, 0), (0, 0), (0, KD)))
        field_spec = jnp.fft.fftn(extended, axes=(1, 2, 3))
        product = jnp.einsum('cexyz,exyz->cxyz', jnp.conj(spectrum), field_spec)
        output = jnp.real(jnp.fft.ifftn(product, axes=(1, 2, 3)))[:, :CX, :CY, :NZ].astype(field.dtype)
        return lax.dynamic_update_slice(result, output, start)

    return lax.fori_loop(0, GX * GY, one_window, jnp.zeros_like(field))


def apply_adjoint(field, psf_bank, psf_ids, weight_ids, list_counts):
    margin = KL // 2
    zero_index = jnp.zeros((), jnp.int32)
    total = jnp.zeros((2, NX + KL, NY + KL, NZ), field.dtype)

    def one_window(index, result):
        index = jnp.asarray(index).astype(jnp.int32)
        row_x = index // GY
        row_y = index % GY
        spectrum = window_spectrum(psf_bank, psf_ids, weight_ids, list_counts, row_x, row_y)
        start = (zero_index, row_x * CX, row_y * CY, zero_index)
        core = lax.dynamic_slice(field, start, (2, CX, CY, NZ))
        core = jnp.pad(core, ((0, 0), (0, KL), (0, KL), (0, KD)))
        field_spec = jnp.fft.fftn(core, axes=(1, 2, 3))
        product = jnp.einsum('cexyz,cxyz->exyz', spectrum, field_spec)
        spread = jnp.real(jnp.fft.ifftn(product, axes=(1, 2, 3)))[:, :, :, :NZ].astype(field.dtype)
        current = lax.dynamic_slice(result, start, (2, CX + KL, CY + KL, NZ))
        return lax.dynamic_update_slice(result, current + spread, start)

    total = lax.fori_loop(0, GX * GY, one_window, total)
    return total[:, margin:margin + NX, margin:margin + NY]


def reference(observed, psf_bank, psf_ids, weight_ids, list_counts):
    solution = jnp.zeros_like(observed)
    residual = observed
    gradient = apply_adjoint(residual, psf_bank, psf_ids, weight_ids, list_counts)
    direction = gradient
    gamma_now = jnp.sum(gradient * gradient)
    for step in range(ITERS):
        imaged = apply_forward(direction, psf_bank, psf_ids, weight_ids, list_counts)
        step_size = gamma_now / jnp.sum(imaged * imaged)
        solution = solution + step_size * direction
        residual = residual - step_size * imaged
        if step + 1 < ITERS:
            gradient = apply_adjoint(residual, psf_bank, psf_ids, weight_ids, list_counts)
            gamma_next = jnp.sum(gradient * gradient)
            direction = gradient + (gamma_next / gamma_now) * direction
            gamma_now = gamma_next
    return solution, residual
```

```python
import functools
import math

import jax
import jax.numpy as jnp
from jax import lax
from jax.experimental import pallas as pl
from jax.experimental.pallas import tpu as pltpu
from jax.sharding import PartitionSpec as P

KL = 32
KD = 16
NW = 16


highest = lax.Precision.HIGH
MESH = pl.DeviceIdType.MESH


def link(src, dst, send_sem, recv_sem, axis, target):
    return pltpu.make_async_remote_copy(
        src_ref=src,
        dst_ref=dst,
        send_sem=send_sem,
        recv_sem=recv_sem,
        device_id={axis: target},
        device_id_type=MESH,
    )


def greet_all(axes):
    barrier = pltpu.get_barrier_semaphore()
    total = 0
    for axis in axes:
        count = lax.axis_size(axis)
        me = lax.axis_index(axis)
        for step in range(1, count):
            pl.semaphore_signal(
                barrier, inc=1, device_id={axis: lax.rem(me + step, count)}, device_id_type=MESH
            )
        total += count - 1
    pl.semaphore_wait(barrier, total)


def blend_kernel(mix, bank, out, parts, arrived, send_sem, recv_sem):
    count = lax.axis_size("sector")
    me = lax.axis_index("sector")
    greet_all(("sector",))

    def partial_sum(window):
        total = mix[window, 0] * bank[0]
        for tile in range(1, bank.shape[0]):
            total = total + mix[window, tile] * bank[tile]
        return total

    copies = []
    for step in range(1, count):
        target = lax.rem(me + step, count)
        parts[step - 1] = partial_sum(target)
        copy = link(
            parts.at[step - 1],
            arrived.at[step - 1],
            send_sem.at[step - 1],
            recv_sem.at[step - 1],
            "sector",
            target,
        )
        copy.start()
        copies.append(copy)
    out[...] = partial_sum(me)
    for step, copy in enumerate(copies):
        copy.wait_recv()
        out[...] += arrived[step]
    for copy in copies:
        copy.wait_send()


def blend(mix, bank):
    rows, width = bank.shape[1:]
    others = lax.axis_size("sector") - 1
    slots = pltpu.VMEM((others, rows, width), jnp.float32)
    return pl.pallas_call(
        blend_kernel,
        out_shape=jax.ShapeDtypeStruct((rows, width), jnp.float32),
        in_specs=[
            pl.BlockSpec(memory_space=pltpu.SMEM),
            pl.BlockSpec(memory_space=pltpu.VMEM),
        ],
        out_specs=pl.BlockSpec(memory_space=pltpu.VMEM),
        scratch_shapes=[
            slots,
            slots,
            pltpu.SemaphoreType.DMA((others,)),
            pltpu.SemaphoreType.DMA((others,)),
        ],
        compiler_params=pltpu.CompilerParams(
            collective_id=0, has_side_effects=True, vmem_limit_bytes=32 * 1024 * 1024
        ),
    )(mix, bank)


def total_kernel(own, out, held, from_win, from_sector, send_sem, recv_sem):
    greet_all(("win", "sector"))
    held[0] = own[...]
    base = 0
    copies = []
    for phase, (axis, landing) in enumerate((("win", from_win), ("sector", from_sector))):
        count = lax.axis_size(axis)
        me = lax.axis_index(axis)
        current = []
        for step in range(1, count):
            slot = base + step - 1
            copy = link(
                held.at[phase],
                landing.at[step - 1],
                send_sem.at[slot],
                recv_sem.at[slot],
                axis,
                lax.rem(me + step, count),
            )
            copy.start()
            current.append(copy)
        base += count - 1
        for copy in current:
            copy.wait_recv()
        total = held[phase]
        for step in range(count - 1):
            total = total + landing[step]
        if phase == 0:
            held[1] = total
        else:
            out[...] = total
        copies += current
    for copy in copies:
        copy.wait_send()


def totals(values):
    rows = len(values)
    tile = jnp.broadcast_to(jnp.stack(values + [values[0]] * (8 - rows))[:, None], (8, 128))
    wins, sectors = lax.axis_size("win") - 1, lax.axis_size("sector") - 1
    summed = pl.pallas_call(
        total_kernel,
        out_shape=jax.ShapeDtypeStruct((8, 128), jnp.float32),
        in_specs=[pl.BlockSpec(memory_space=pltpu.VMEM)],
        out_specs=pl.BlockSpec(memory_space=pltpu.VMEM),
        scratch_shapes=[
            pltpu.VMEM((2, 8, 128), jnp.float32),
            pltpu.VMEM((wins, 8, 128), jnp.float32),
            pltpu.VMEM((sectors, 8, 128), jnp.float32),
            pltpu.SemaphoreType.DMA((wins + sectors,)),
            pltpu.SemaphoreType.DMA((wins + sectors,)),
        ],
        compiler_params=pltpu.CompilerParams(collective_id=1, has_side_effects=True),
    )(tile)
    return [summed[row, 0] for row in range(rows)]


def fold_kernel(spread, grad, ext, win_in, sec_in, mid, send_sem, recv_sem):
    comps, core_x, core_y = grad.shape[:3]
    rim = KL // 2
    rows = (pl.ds(0, rim), pl.ds(rim, core_x), pl.ds(rim + core_x, rim))
    cols = (pl.ds(0, rim), pl.ds(rim, core_y), pl.ds(rim + core_y, rim))
    place = {axis: lax.axis_index(axis) for axis in ("sector", "win")}
    exists = {}
    for axis, me in place.items():
        exists[axis, -1] = me > 0
        exists[axis, 1] = me < lax.axis_size(axis) - 1

    barrier = pltpu.get_barrier_semaphore()
    for (axis, way), there in exists.items():

        @pl.when(there)
        def _():
            pl.semaphore_signal(
                barrier, inc=1, device_id={axis: place[axis] + way}, device_id_type=MESH
            )

    pl.semaphore_wait(barrier, sum(there.astype(jnp.int32) for there in exists.values()))

    started = []
    slots = {}

    def copy_of(key, axis, way, src, dst):
        slot = slots.setdefault(key, len(slots))
        return link(src, dst, send_sem.at[slot], recv_sem.at[slot], axis, place[axis] + way)

    def send(key, axis, way, src, dst):
        @pl.when(exists[axis, way])
        def _():
            copy_of(key, axis, way, src, dst).start()

        started.append((key, axis, way, src, dst))

    def receive(key, axis, way, src, dst, then=None):
        @pl.when(exists[axis, -way])
        def _():
            copy_of(key, axis, way, src, dst).wait_recv()
            if then is not None:
                then()

    ways = ((0, -1), (1, 1))

    def rim_of(c, part, side):
        return (
            spread.at[c, rows[part], cols[2 * side]],
            win_in.at[side, c, rows[part]],
        )

    for c in range(comps):
        for part in (0, 2, 1):
            for side, way in ways:
                send(("rim", c, part, side), "win", way, *rim_of(c, part, side))
    for c in range(comps):
        for part in (0, 2, 1):
            mid[c, rows[part]] = spread[c, rows[part], cols[1]]
            for side, way in ways:

                def add():
                    mid[c, rows[part]] += win_in[side, c, rows[part]]

                receive(("rim", c, part, side), "win", way, *rim_of(c, part, side), add)
            if part != 1:
                side = part // 2
                send(
                    ("edge", c, side), "sector", ways[side][1], mid.at[c, rows[part]], sec_in.at[side, c]
                )

    def around(c, side):
        return ext.at[c, rows[1], cols[1]], ext.at[c, rows[2 - 2 * side], cols[1]]

    def beside(c, part, side):
        return ext.at[c, rows[part], cols[1]], ext.at[c, rows[part], cols[2 - 2 * side]]

    for c in range(comps):
        grad[c] = mid[c, rows[1]]
        for side, way in ways:

            def add_edge():
                grad[c] += sec_in[side, c]

            receive(
                ("edge", c, side), "sector", way, mid.at[c, rows[2 * side]], sec_in.at[side, c], add_edge
            )
        ext[c, rows[1], cols[1]] = grad[c]
        for side, way in ways:
            send(("around", c, side), "sector", way, *around(c, side))
        for side, way in ways:
            send(("beside", c, 1, side), "win", way, *beside(c, 1, side))

    for c in range(comps):
        for side, way in ways:
            part = 2 - 2 * side

            def pass_on():
                for side_y, way_y in ways:

                    @pl.when(exists["win", way_y])
                    def _():
                        copy_of(
                            ("beside", c, part, side_y), "win", way_y, *beside(c, part, side_y)
                        ).start()

            receive(("around", c, side), "sector", way, *around(c, side), pass_on)

            @pl.when(jnp.logical_not(exists["sector", -way]))
            def _():
                ext[c, rows[part]] = jnp.zeros((rim,) + ext.shape[2:], jnp.float32)

        for side, way in ways:
            missing = jnp.logical_not(exists["win", -way])

            @pl.when(missing)
            def _():
                for part, height in ((0, rim), (1, core_x), (2, rim)):
                    ext[c, rows[part], cols[2 - 2 * side]] = jnp.zeros(
                        (height, rim, ext.shape[3]), jnp.float32
                    )

    for c in range(comps):
        for side, way in ways:
            receive(("beside", c, 1, side), "win", way, *beside(c, 1, side))
        for side_x, way_x in ways:
            part = 2 - 2 * side_x

            @pl.when(exists["sector", -way_x])
            def _():
                for side, way in ways:
                    receive(("beside", c, part, side), "win", way, *beside(c, part, side))

                    @pl.when(exists["win", way])
                    def _():
                        copy_of(
                            ("beside", c, part, side), "win", way, *beside(c, part, side)
                        ).wait_send()

    for key, axis, way, src, dst in started:

        @pl.when(exists[axis, way])
        def _():
            copy_of(key, axis, way, src, dst).wait_send()


def fold_and_extend(spread, core_x, core_y):
    comps, wide_x, wide_y, depth = spread.shape
    rim = KL // 2
    count = comps * (6 + 2 + 2 + 6)
    vmem = pl.BlockSpec(memory_space=pltpu.VMEM)
    return pl.pallas_call(
        fold_kernel,
        out_shape=(
            jax.ShapeDtypeStruct((comps, core_x, core_y, depth), jnp.float32),
            jax.ShapeDtypeStruct(spread.shape, jnp.float32),
        ),
        in_specs=[vmem],
        out_specs=(vmem, vmem),
        scratch_shapes=[
            pltpu.VMEM((2, comps, wide_x, rim, depth), jnp.float32),
            pltpu.VMEM((2, comps, rim, core_y, depth), jnp.float32),
            pltpu.VMEM((comps, wide_x, core_y, depth), jnp.float32),
            pltpu.SemaphoreType.DMA((count,)),
            pltpu.SemaphoreType.DMA((count,)),
        ],
        compiler_params=pltpu.CompilerParams(
            collective_id=2, has_side_effects=True, vmem_limit_bytes=40 * 1024 * 1024
        ),
    )(spread)


def index_angles(row_count, col_count, length, offset):
    row_index = (jnp.arange(row_count, dtype=jnp.int32)[:, None] + offset) % length
    col_index = jnp.arange(col_count, dtype=jnp.int32)[None, :]
    phase = row_index * col_index % length
    angle = phase.astype(jnp.float32) * (2.0 * math.pi / length)
    return (jnp.cos(angle), jnp.sin(angle))


def half_forward(row_count, length):
    cos_part, sin_part = index_angles(row_count, length // 2 + 1, length, 0)
    return jnp.stack([cos_part, -sin_part], axis=1)


def full_forward(row_count, length, offset):
    cos_part, sin_part = index_angles(row_count, length, length, offset)
    real_rows = jnp.stack([cos_part, -sin_part], axis=1)
    imag_rows = jnp.stack([sin_part, cos_part], axis=1)
    return jnp.stack([real_rows, imag_rows], axis=0)


def full_inverse(length, out_count):
    cos_part, sin_part = index_angles(length, out_count, length, 0)
    real_rows = jnp.stack([cos_part, sin_part], axis=1)
    imag_rows = jnp.stack([-sin_part, cos_part], axis=1)
    return jnp.stack([real_rows, imag_rows], axis=0)


def half_inverse(length, out_count):
    half_count = length // 2 + 1
    cos_part, sin_part = index_angles(half_count, out_count, length, 0)
    frequency = jnp.arange(half_count, dtype=jnp.int32)
    edge = (frequency == 0) | (frequency == length // 2)
    weights = jnp.where(edge, 1.0, 2.0)[:, None]
    return jnp.stack([cos_part * weights, -sin_part * weights], axis=0)


def spectrum_of(values_in, width_x, width_y, length_z, depth_offset):
    rows_x, rows_y, depth = (values_in.shape[1], values_in.shape[2], values_in.shape[3])
    along_x = jnp.einsum(
        "xrj,mxyz->rjmyz", half_forward(rows_x, width_x), values_in, precision=highest
    )
    along_y = jnp.einsum(
        "rysj,rxmyz->sjxmz", full_forward(rows_y, width_y, 0), along_x, precision=highest
    )
    return jnp.einsum(
        "ryxmz,rzsk->yxmsk", along_y, full_forward(depth, length_z, depth_offset), precision=highest
    )


def values_of(spectrum, out_x, out_y, out_z, width_x, length_z):
    width_y = spectrum.shape[0]
    depth_back = jnp.einsum(
        "yxmsk,skrz->yxmrz", spectrum, full_inverse(length_z, out_z), precision=highest
    )
    table_y = full_inverse(width_y, out_y).transpose(1, 0, 2, 3)
    lateral_y = jnp.einsum("arsy,axmrz->syxmz", table_y, depth_back, precision=highest)
    lateral_x = jnp.einsum(
        "sjx,syjmz->xymz", half_inverse(width_x, out_x), lateral_y, precision=highest
    )
    scaling = 1.0 / (width_x * width_y * length_z)
    return (lateral_x * scaling).transpose(2, 0, 1, 3)


def kernel_spectrum(flat_kernel, width_x, width_y, length_z):
    kernel = flat_kernel.reshape(4, KD, KL, KL).transpose(0, 2, 3, 1)
    spectrum = spectrum_of(kernel, width_x, width_y, length_z, -(KD // 2))
    return spectrum.reshape(spectrum.shape[0], spectrum.shape[1], 2, 2, 2, spectrum.shape[4])


def correlate(kernel_spec, spectrum):
    kernel_real, kernel_imag = (kernel_spec[..., 0, :], kernel_spec[..., 1, :])
    field_real = spectrum[:, :, None, :, 0, :]
    field_imag = spectrum[:, :, None, :, 1, :]
    real_part = jnp.sum(kernel_real * field_real + kernel_imag * field_imag, axis=3)
    imag_part = jnp.sum(kernel_real * field_imag - kernel_imag * field_real, axis=3)
    return jnp.stack([real_part, imag_part], axis=3)


def convolve(kernel_spec, spectrum):
    kernel_real, kernel_imag = (kernel_spec[..., 0, :], kernel_spec[..., 1, :])
    field_real = spectrum[:, :, :, None, 0, :]
    field_imag = spectrum[:, :, :, None, 1, :]
    real_part = jnp.sum(kernel_real * field_real - kernel_imag * field_imag, axis=2)
    imag_part = jnp.sum(kernel_real * field_imag + kernel_imag * field_real, axis=2)
    return jnp.stack([real_part, imag_part], axis=3)


def hessian_image(extended, kernel_spec, core_x, core_y, length_z):
    width_x, width_y = (extended.shape[1], extended.shape[2])
    spectrum = spectrum_of(extended, width_x, width_y, length_z, 0)
    return values_of(
        correlate(kernel_spec, spectrum), core_x, core_y, extended.shape[3], width_x, length_z
    )


def adjoint_image(values_in, kernel_spec, length_z):
    rows_x, rows_y, depth = (values_in.shape[1], values_in.shape[2], values_in.shape[3])
    width_x, width_y = (rows_x + KL, rows_y + KL)
    spectrum = spectrum_of(values_in, width_x, width_y, length_z, 0)
    spread = values_of(convolve(kernel_spec, spectrum), width_x, width_y, depth, width_x, length_z)
    return fold_and_extend(spread, rows_x, rows_y)


def per_device(observed, psf_bank, psf_ids, weight_ids, list_counts):
    shard_rows = psf_bank.shape[0]
    own_ids = psf_ids[:, 0, :]
    in_list = (jnp.arange(own_ids.shape[1], dtype=jnp.int32)[None, :] < list_counts).astype(
        jnp.float32
    )
    factors = in_list * (weight_ids[:, 0, :].astype(jnp.float32) + 1.0) / NW
    sector_index = lax.axis_index("sector")
    bank_total = shard_rows * lax.axis_size("sector")
    matches = (
        own_ids[:, :, None] == jnp.arange(bank_total, dtype=jnp.int32)[None, None, :]
    ).astype(jnp.float32)
    mixing = jnp.sum(matches * factors[:, :, None], axis=1)
    own_mixing = lax.dynamic_slice_in_dim(mixing, sector_index * shard_rows, shard_rows, 1)
    tiles = psf_bank.reshape(shard_rows, 4 * KD, KL * KL)
    blended = blend(own_mixing, tiles)
    core_x, core_y = observed.shape[1:3]
    length_z = observed.shape[3] + KD
    kernel_spec = kernel_spectrum(blended, core_x + KL, core_y + KL, length_z)
    gradient, around = adjoint_image(observed, kernel_spec, length_z)
    imaged = hessian_image(around, kernel_spec, core_x, core_y, length_z)
    turned, around = adjoint_image(imaged, kernel_spec, length_z)
    turned_image = hessian_image(around, kernel_spec, core_x, core_y, length_z)
    gamma, energy, cross, curve, mixed, second = totals(
        [
            jnp.sum(gradient * gradient),
            jnp.sum(imaged * imaged),
            jnp.sum(gradient * turned),
            jnp.sum(turned * turned),
            jnp.sum(imaged * turned_image),
            jnp.sum(turned_image * turned_image),
        ]
    )
    step = gamma / energy
    gamma_next = gamma - 2.0 * step * cross + step * step * curve
    keep = 1.0 + gamma_next / gamma
    next_energy = keep * keep * energy - 2.0 * keep * step * mixed + step * step * second
    next_step = gamma_next / next_energy
    along = step + next_step * keep
    across = next_step * step
    return (
        along * gradient - across * turned,
        observed - along * imaged + across * turned_image,
    )


def solution(mesh):
    placed = (
        P(None, "sector", "win", None),
        P("sector", None, None, None, None),
        P(None, "win", None),
        P(None, "win", None),
        P(None, "win"),
    )
    return jax.shard_map(
        per_device,
        mesh=mesh,
        in_specs=placed,
        out_specs=(P(None, "sector", "win", None), P(None, "sector", "win", None)),
        check_vma=False,
    )
```

```python
import functools
import math

import jax
import jax.numpy as jnp
import numpy as np
from jax import lax
from jax.experimental import pallas as pl
from jax.experimental.pallas import tpu as pltpu
from jax.sharding import PartitionSpec as P

KL = 32
KD = 16
NW = 16


highest = lax.Precision.HIGH
MESH = pl.DeviceIdType.MESH


def link(src, dst, send_sem, recv_sem, axis, target):
    return pltpu.make_async_remote_copy(
        src_ref=src,
        dst_ref=dst,
        send_sem=send_sem,
        recv_sem=recv_sem,
        device_id={axis: target},
        device_id_type=MESH,
    )


def greet_all(axes):
    barrier = pltpu.get_barrier_semaphore()
    total = 0
    for axis in axes:
        count = lax.axis_size(axis)
        me = lax.axis_index(axis)
        for step in range(1, count):
            pl.semaphore_signal(
                barrier, inc=1, device_id={axis: lax.rem(me + step, count)}, device_id_type=MESH
            )
        total += count - 1
    pl.semaphore_wait(barrier, total)


def blend_kernel(mix, bank, out, parts, arrived, send_sem, recv_sem):
    count = lax.axis_size("sector")
    me = lax.axis_index("sector")
    greet_all(("sector",))

    def partial_sum(window):
        total = mix[window, 0] * bank[0]
        for tile in range(1, bank.shape[0]):
            total = total + mix[window, tile] * bank[tile]
        return total

    copies = []
    for step in range(1, count):
        target = lax.rem(me + step, count)
        parts[step - 1] = partial_sum(target)
        copy = link(
            parts.at[step - 1],
            arrived.at[step - 1],
            send_sem.at[step - 1],
            recv_sem.at[step - 1],
            "sector",
            target,
        )
        copy.start()
        copies.append(copy)
    out[...] = partial_sum(me)
    for step, copy in enumerate(copies):
        copy.wait_recv()
        out[...] += arrived[step]
    for copy in copies:
        copy.wait_send()


def blend(mix, bank):
    rows, width = bank.shape[1:]
    others = lax.axis_size("sector") - 1
    slots = pltpu.VMEM((others, rows, width), jnp.float32)
    return pl.pallas_call(
        blend_kernel,
        out_shape=jax.ShapeDtypeStruct((rows, width), jnp.float32),
        in_specs=[
            pl.BlockSpec(memory_space=pltpu.SMEM),
            pl.BlockSpec(memory_space=pltpu.VMEM),
        ],
        out_specs=pl.BlockSpec(memory_space=pltpu.VMEM),
        scratch_shapes=[
            slots,
            slots,
            pltpu.SemaphoreType.DMA((others,)),
            pltpu.SemaphoreType.DMA((others,)),
        ],
        compiler_params=pltpu.CompilerParams(
            collective_id=0, has_side_effects=True, vmem_limit_bytes=32 * 1024 * 1024
        ),
    )(mix, bank)


def finish_kernel(
    grad, turned, observed, imaged, second, solved, left, held, from_win, from_sector, send_sem, recv_sem
):
    pairs = (
        (grad, grad),
        (imaged, imaged),
        (grad, turned),
        (turned, turned),
        (imaged, second),
        (second, second),
    )
    held[0] = jnp.zeros(held.shape[1:], jnp.float32)
    for row, (one, other) in enumerate(pairs):
        lanes = jnp.sum(one[...] * other[...], axis=(0, 1))
        held[0, row : row + 1] = jnp.sum(lanes, axis=0, keepdims=True)
    greet_all(("win", "sector"))
    base = 0
    copies = []
    for phase, (axis, landing) in enumerate((("win", from_win), ("sector", from_sector))):
        count = lax.axis_size(axis)
        me = lax.axis_index(axis)
        current = []
        for step in range(1, count):
            slot = base + step - 1
            copy = link(
                held.at[phase],
                landing.at[step - 1],
                send_sem.at[slot],
                recv_sem.at[slot],
                axis,
                lax.rem(me + step, count),
            )
            copy.start()
            current.append(copy)
        base += count - 1
        for copy in current:
            copy.wait_recv()
        total = held[phase]
        for step in range(count - 1):
            total = total + landing[step]
        if phase == 0:
            held[1] = total
        copies += current
    sums = [jnp.sum(total[row : row + 1], axis=1, keepdims=True) for row in range(len(pairs))]
    gamma, energy, cross, curve, mixed, last = sums
    step = gamma / energy
    gamma_next = gamma - 2.0 * step * cross + step * step * curve
    keep = 1.0 + gamma_next / gamma
    next_energy = keep * keep * energy - 2.0 * keep * step * mixed + step * step * last
    next_step = gamma_next / next_energy
    along = step + next_step * keep
    across = next_step * step
    for c in range(grad.shape[0]):
        for x in range(grad.shape[1]):
            solved[c, x] = along * grad[c, x] - across * turned[c, x]
            left[c, x] = observed[c, x] - along * imaged[c, x] + across * second[c, x]
    for copy in copies:
        copy.wait_send()


def finish(*fields):
    wins, sectors = lax.axis_size("win") - 1, lax.axis_size("sector") - 1
    vmem = pl.BlockSpec(memory_space=pltpu.VMEM)
    result = jax.ShapeDtypeStruct(fields[0].shape, jnp.float32)
    return pl.pallas_call(
        finish_kernel,
        out_shape=(result, result),
        in_specs=[vmem] * len(fields),
        out_specs=(vmem, vmem),
        scratch_shapes=[
            pltpu.VMEM((2, 8, 128), jnp.float32),
            pltpu.VMEM((wins, 8, 128), jnp.float32),
            pltpu.VMEM((sectors, 8, 128), jnp.float32),
            pltpu.SemaphoreType.DMA((wins + sectors,)),
            pltpu.SemaphoreType.DMA((wins + sectors,)),
        ],
        compiler_params=pltpu.CompilerParams(
            collective_id=1, has_side_effects=True, vmem_limit_bytes=32 * 1024 * 1024
        ),
    )(*fields)


def fold_kernel(spread, grad, ext, win_in, sec_in, mid, send_sem, recv_sem):
    comps, core_x, core_y = grad.shape[:3]
    rim = KL // 2
    rows = (pl.ds(0, rim), pl.ds(rim, core_x), pl.ds(rim + core_x, rim))
    cols = (pl.ds(0, rim), pl.ds(rim, core_y), pl.ds(rim + core_y, rim))
    place = {axis: lax.axis_index(axis) for axis in ("sector", "win")}
    exists = {}
    for axis, me in place.items():
        exists[axis, -1] = me > 0
        exists[axis, 1] = me < lax.axis_size(axis) - 1

    barrier = pltpu.get_barrier_semaphore()
    for (axis, way), there in exists.items():

        @pl.when(there)
        def _():
            pl.semaphore_signal(
                barrier, inc=1, device_id={axis: place[axis] + way}, device_id_type=MESH
            )

    pl.semaphore_wait(barrier, sum(there.astype(jnp.int32) for there in exists.values()))

    started = []
    slots = {}

    def copy_of(key, axis, way, src, dst):
        slot = slots.setdefault(key, len(slots))
        return link(src, dst, send_sem.at[slot], recv_sem.at[slot], axis, place[axis] + way)

    def send(key, axis, way, src, dst):
        @pl.when(exists[axis, way])
        def _():
            copy_of(key, axis, way, src, dst).start()

        started.append((key, axis, way, src, dst))

    def receive(key, axis, way, src, dst, then=None):
        @pl.when(exists[axis, -way])
        def _():
            copy_of(key, axis, way, src, dst).wait_recv()
            if then is not None:
                then()

    ways = ((0, -1), (1, 1))

    def rim_of(c, part, side):
        return (
            spread.at[c, rows[part], cols[2 * side]],
            win_in.at[side, c, rows[part]],
        )

    for c in range(comps):
        for part in (0, 2, 1):
            for side, way in ways:
                send(("rim", c, part, side), "win", way, *rim_of(c, part, side))
    for c in range(comps):
        for part in (0, 2, 1):
            mid[c, rows[part]] = spread[c, rows[part], cols[1]]
            for side, way in ways:

                def add():
                    mid[c, rows[part]] += win_in[side, c, rows[part]]

                receive(("rim", c, part, side), "win", way, *rim_of(c, part, side), add)
            if part != 1:
                side = part // 2
                send(
                    ("edge", c, side), "sector", ways[side][1], mid.at[c, rows[part]], sec_in.at[side, c]
                )

    def around(c, side):
        return ext.at[c, rows[1], cols[1]], ext.at[c, rows[2 - 2 * side], cols[1]]

    def beside(c, part, side):
        return ext.at[c, rows[part], cols[1]], ext.at[c, rows[part], cols[2 - 2 * side]]

    for c in range(comps):
        grad[c] = mid[c, rows[1]]
        for side, way in ways:

            def add_edge():
                grad[c] += sec_in[side, c]

            receive(
                ("edge", c, side), "sector", way, mid.at[c, rows[2 * side]], sec_in.at[side, c], add_edge
            )
        ext[c, rows[1], cols[1]] = grad[c]
        for side, way in ways:
            send(("around", c, side), "sector", way, *around(c, side))
        for side, way in ways:
            send(("beside", c, 1, side), "win", way, *beside(c, 1, side))

    for c in range(comps):
        for side, way in ways:
            part = 2 - 2 * side

            def pass_on():
                for side_y, way_y in ways:

                    @pl.when(exists["win", way_y])
                    def _():
                        copy_of(
                            ("beside", c, part, side_y), "win", way_y, *beside(c, part, side_y)
                        ).start()

            receive(("around", c, side), "sector", way, *around(c, side), pass_on)

            @pl.when(jnp.logical_not(exists["sector", -way]))
            def _():
                ext[c, rows[part]] = jnp.zeros((rim,) + ext.shape[2:], jnp.float32)

        for side, way in ways:
            missing = jnp.logical_not(exists["win", -way])

            @pl.when(missing)
            def _():
                for part, height in ((0, rim), (1, core_x), (2, rim)):
                    ext[c, rows[part], cols[2 - 2 * side]] = jnp.zeros(
                        (height, rim, ext.shape[3]), jnp.float32
                    )

    for c in range(comps):
        for side, way in ways:
            receive(("beside", c, 1, side), "win", way, *beside(c, 1, side))
        for side_x, way_x in ways:
            part = 2 - 2 * side_x

            @pl.when(exists["sector", -way_x])
            def _():
                for side, way in ways:
                    receive(("beside", c, part, side), "win", way, *beside(c, part, side))

                    @pl.when(exists["win", way])
                    def _():
                        copy_of(
                            ("beside", c, part, side), "win", way, *beside(c, part, side)
                        ).wait_send()

    for key, axis, way, src, dst in started:

        @pl.when(exists[axis, way])
        def _():
            copy_of(key, axis, way, src, dst).wait_send()


def fold_and_extend(spread, core_x, core_y):
    comps, wide_x, wide_y, depth = spread.shape
    rim = KL // 2
    count = comps * (6 + 2 + 2 + 6)
    vmem = pl.BlockSpec(memory_space=pltpu.VMEM)
    return pl.pallas_call(
        fold_kernel,
        out_shape=(
            jax.ShapeDtypeStruct((comps, core_x, core_y, depth), jnp.float32),
            jax.ShapeDtypeStruct(spread.shape, jnp.float32),
        ),
        in_specs=[vmem],
        out_specs=(vmem, vmem),
        scratch_shapes=[
            pltpu.VMEM((2, comps, wide_x, rim, depth), jnp.float32),
            pltpu.VMEM((2, comps, rim, core_y, depth), jnp.float32),
            pltpu.VMEM((comps, wide_x, core_y, depth), jnp.float32),
            pltpu.SemaphoreType.DMA((count,)),
            pltpu.SemaphoreType.DMA((count,)),
        ],
        compiler_params=pltpu.CompilerParams(
            collective_id=2, has_side_effects=True, vmem_limit_bytes=40 * 1024 * 1024
        ),
    )(spread)


def index_angles(row_count, col_count, length, offset):
    row_index = (np.arange(row_count, dtype=np.int64)[:, None] + offset) % length
    col_index = np.arange(col_count, dtype=np.int64)[None, :]
    phase = row_index * col_index % length
    angle = phase * (2.0 * math.pi / length)
    return (np.cos(angle).astype(np.float32), np.sin(angle).astype(np.float32))


def half_forward(row_count, length):
    cos_part, sin_part = index_angles(row_count, length // 2 + 1, length, 0)
    return np.stack([cos_part, -sin_part], axis=1)


def full_forward(row_count, length, offset):
    cos_part, sin_part = index_angles(row_count, length, length, offset)
    real_rows = np.stack([cos_part, -sin_part], axis=1)
    imag_rows = np.stack([sin_part, cos_part], axis=1)
    return np.stack([real_rows, imag_rows], axis=0)


def full_inverse(length, out_count):
    cos_part, sin_part = index_angles(length, out_count, length, 0)
    real_rows = np.stack([cos_part, sin_part], axis=1)
    imag_rows = np.stack([-sin_part, cos_part], axis=1)
    return np.stack([real_rows, imag_rows], axis=0)


def half_inverse(length, out_count):
    half_count = length // 2 + 1
    cos_part, sin_part = index_angles(half_count, out_count, length, 0)
    frequency = np.arange(half_count, dtype=np.int64)
    edge = (frequency == 0) | (frequency == length // 2)
    weights = np.where(edge, 1.0, 2.0).astype(np.float32)[:, None]
    return np.stack([cos_part * weights, -sin_part * weights], axis=0)


def spectrum_of(values_in, width_x, width_y, length_z, depth_offset):
    rows_x, rows_y, depth = (values_in.shape[1], values_in.shape[2], values_in.shape[3])
    along_x = jnp.einsum(
        "xrj,mxyz->rjmyz", half_forward(rows_x, width_x), values_in, precision=highest
    )
    along_y = jnp.einsum(
        "rysj,rxmyz->sjxmz", full_forward(rows_y, width_y, 0), along_x, precision=highest
    )
    return jnp.einsum(
        "ryxmz,rzsk->yxmsk", along_y, full_forward(depth, length_z, depth_offset), precision=highest
    )


def values_of(spectrum, out_x, out_y, out_z, width_x, length_z):
    width_y = spectrum.shape[0]
    depth_back = jnp.einsum(
        "yxmsk,skrz->yxmrz", spectrum, full_inverse(length_z, out_z), precision=highest
    )
    table_y = full_inverse(width_y, out_y).transpose(1, 0, 2, 3)
    lateral_y = jnp.einsum("arsy,axmrz->syxmz", table_y, depth_back, precision=highest)
    lateral_x = jnp.einsum(
        "sjx,syjmz->xymz", half_inverse(width_x, out_x), lateral_y, precision=highest
    )
    scaling = 1.0 / (width_x * width_y * length_z)
    return (lateral_x * scaling).transpose(2, 0, 1, 3)


def kernel_spectrum(flat_kernel, width_x, width_y, length_z):
    kernel = flat_kernel.reshape(4, KD, KL, KL).transpose(0, 2, 3, 1)
    spectrum = spectrum_of(kernel, width_x, width_y, length_z, -(KD // 2))
    return spectrum.reshape(spectrum.shape[0], spectrum.shape[1], 2, 2, 2, spectrum.shape[4])


def correlate(kernel_spec, spectrum):
    kernel_real, kernel_imag = (kernel_spec[..., 0, :], kernel_spec[..., 1, :])
    field_real = spectrum[:, :, None, :, 0, :]
    field_imag = spectrum[:, :, None, :, 1, :]
    real_part = jnp.sum(kernel_real * field_real + kernel_imag * field_imag, axis=3)
    imag_part = jnp.sum(kernel_real * field_imag - kernel_imag * field_real, axis=3)
    return jnp.stack([real_part, imag_part], axis=3)


def convolve(kernel_spec, spectrum):
    kernel_real, kernel_imag = (kernel_spec[..., 0, :], kernel_spec[..., 1, :])
    field_real = spectrum[:, :, :, None, 0, :]
    field_imag = spectrum[:, :, :, None, 1, :]
    real_part = jnp.sum(kernel_real * field_real - kernel_imag * field_imag, axis=2)
    imag_part = jnp.sum(kernel_real * field_imag + kernel_imag * field_real, axis=2)
    return jnp.stack([real_part, imag_part], axis=3)


def hessian_image(extended, kernel_spec, core_x, core_y, length_z):
    width_x, width_y = (extended.shape[1], extended.shape[2])
    spectrum = spectrum_of(extended, width_x, width_y, length_z, 0)
    return values_of(
        correlate(kernel_spec, spectrum), core_x, core_y, extended.shape[3], width_x, length_z
    )


def adjoint_image(values_in, kernel_spec, length_z):
    rows_x, rows_y, depth = (values_in.shape[1], values_in.shape[2], values_in.shape[3])
    width_x, width_y = (rows_x + KL, rows_y + KL)
    spectrum = spectrum_of(values_in, width_x, width_y, length_z, 0)
    spread = values_of(convolve(kernel_spec, spectrum), width_x, width_y, depth, width_x, length_z)
    return fold_and_extend(spread, rows_x, rows_y)


def per_device(observed, psf_bank, psf_ids, weight_ids, list_counts):
    shard_rows = psf_bank.shape[0]
    own_ids = psf_ids[:, 0, :]
    in_list = (jnp.arange(own_ids.shape[1], dtype=jnp.int32)[None, :] < list_counts).astype(
        jnp.float32
    )
    factors = in_list * (weight_ids[:, 0, :].astype(jnp.float32) + 1.0) / NW
    sector_index = lax.axis_index("sector")
    bank_total = shard_rows * lax.axis_size("sector")
    matches = (
        own_ids[:, :, None] == jnp.arange(bank_total, dtype=jnp.int32)[None, None, :]
    ).astype(jnp.float32)
    mixing = jnp.sum(matches * factors[:, :, None], axis=1)
    own_mixing = lax.dynamic_slice_in_dim(mixing, sector_index * shard_rows, shard_rows, 1)
    tiles = psf_bank.reshape(shard_rows, 4 * KD, KL * KL)
    blended = blend(own_mixing, tiles)
    core_x, core_y = observed.shape[1:3]
    length_z = observed.shape[3] + KD
    kernel_spec = kernel_spectrum(blended, core_x + KL, core_y + KL, length_z)
    gradient, around = adjoint_image(observed, kernel_spec, length_z)
    imaged = hessian_image(around, kernel_spec, core_x, core_y, length_z)
    turned, around = adjoint_image(imaged, kernel_spec, length_z)
    turned_image = hessian_image(around, kernel_spec, core_x, core_y, length_z)
    return finish(gradient, turned, observed, imaged, turned_image)


def solution(mesh):
    placed = (
        P(None, "sector", "win", None),
        P("sector", None, None, None, None),
        P(None, "win", None),
        P(None, "win", None),
        P(None, "win"),
    )
    return jax.shard_map(
        per_device,
        mesh=mesh,
        in_specs=placed,
        out_specs=(P(None, "sector", "win", None), P(None, "sector", "win", None)),
        check_vma=False,
    )
```

```python
import functools
import math

import jax
import jax.numpy as jnp
import numpy as np
from jax import lax
from jax.experimental import pallas as pl
from jax.experimental.pallas import tpu as pltpu
from jax.sharding import PartitionSpec as P

KL = 32
KD = 16
NW = 16


highest = lax.Precision.HIGH
MESH = pl.DeviceIdType.MESH


def link(src, dst, send_sem, recv_sem, axis, target):
    return pltpu.make_async_remote_copy(
        src_ref=src,
        dst_ref=dst,
        send_sem=send_sem,
        recv_sem=recv_sem,
        device_id={axis: target},
        device_id_type=MESH,
    )


def greet_all(axes):
    barrier = pltpu.get_barrier_semaphore()
    total = 0
    for axis in axes:
        count = lax.axis_size(axis)
        me = lax.axis_index(axis)
        for step in range(1, count):
            pl.semaphore_signal(
                barrier, inc=1, device_id={axis: lax.rem(me + step, count)}, device_id_type=MESH
            )
        total += count - 1
    pl.semaphore_wait(barrier, total)


def blend_kernel(ids, levels, counts, bank, out, parts, arrived, send_sem, recv_sem):
    count = lax.axis_size("sector")
    me = lax.axis_index("sector")
    greet_all(("sector",))

    def factor(window, tile):
        total = jnp.float32(0.0)
        for entry in range(ids.shape[2]):
            named = ids[window, 0, entry] == me * bank.shape[0] + tile
            live = jnp.logical_and(named, entry < counts[window, 0])
            level = (levels[window, 0, entry].astype(jnp.float32) + 1.0) * (1.0 / NW)
            total = total + jnp.where(live, level, 0.0)
        return total

    def partial_sum(window):
        total = factor(window, 0) * bank[0]
        for tile in range(1, bank.shape[0]):
            total = total + factor(window, tile) * bank[tile]
        return total

    copies = []
    for step in range(1, count):
        target = lax.rem(me + step, count)
        parts[step - 1] = partial_sum(target)
        copy = link(
            parts.at[step - 1],
            arrived.at[step - 1],
            send_sem.at[step - 1],
            recv_sem.at[step - 1],
            "sector",
            target,
        )
        copy.start()
        copies.append(copy)
    out[...] = partial_sum(me)
    for step, copy in enumerate(copies):
        copy.wait_recv()
        out[...] += arrived[step]
    for copy in copies:
        copy.wait_send()


def blend(ids, levels, counts, bank):
    rows, width = bank.shape[1:]
    others = lax.axis_size("sector") - 1
    slots = pltpu.VMEM((others, rows, width), jnp.float32)
    return pl.pallas_call(
        blend_kernel,
        out_shape=jax.ShapeDtypeStruct((rows, width), jnp.float32),
        in_specs=[
            pl.BlockSpec(memory_space=pltpu.SMEM),
            pl.BlockSpec(memory_space=pltpu.SMEM),
            pl.BlockSpec(memory_space=pltpu.SMEM),
            pl.BlockSpec(memory_space=pltpu.VMEM),
        ],
        out_specs=pl.BlockSpec(memory_space=pltpu.VMEM),
        scratch_shapes=[
            slots,
            slots,
            pltpu.SemaphoreType.DMA((others,)),
            pltpu.SemaphoreType.DMA((others,)),
        ],
        compiler_params=pltpu.CompilerParams(
            collective_id=0, has_side_effects=True, vmem_limit_bytes=32 * 1024 * 1024
        ),
    )(ids, levels, counts, bank)


def finish_kernel(
    grad, turned, observed, imaged, second, solved, left, held, from_win, from_sector, send_sem, recv_sem
):
    pairs = (
        (grad, grad),
        (imaged, imaged),
        (grad, turned),
        (turned, turned),
        (imaged, second),
        (second, second),
    )
    held[0] = jnp.zeros(held.shape[1:], jnp.float32)
    for row, (one, other) in enumerate(pairs):
        lanes = jnp.sum(one[...] * other[...], axis=(0, 1))
        held[0, row : row + 1] = jnp.sum(lanes, axis=0, keepdims=True)
    greet_all(("win", "sector"))
    base = 0
    copies = []
    for phase, (axis, landing) in enumerate((("win", from_win), ("sector", from_sector))):
        count = lax.axis_size(axis)
        me = lax.axis_index(axis)
        current = []
        for step in range(1, count):
            slot = base + step - 1
            copy = link(
                held.at[phase],
                landing.at[step - 1],
                send_sem.at[slot],
                recv_sem.at[slot],
                axis,
                lax.rem(me + step, count),
            )
            copy.start()
            current.append(copy)
        base += count - 1
        for copy in current:
            copy.wait_recv()
        total = held[phase]
        for step in range(count - 1):
            total = total + landing[step]
        if phase == 0:
            held[1] = total
        copies += current
    sums = [jnp.sum(total[row : row + 1], axis=1, keepdims=True) for row in range(len(pairs))]
    gamma, energy, cross, curve, mixed, last = sums
    step = gamma / energy
    gamma_next = gamma - 2.0 * step * cross + step * step * curve
    keep = 1.0 + gamma_next / gamma
    next_energy = keep * keep * energy - 2.0 * keep * step * mixed + step * step * last
    next_step = gamma_next / next_energy
    along = step + next_step * keep
    across = next_step * step
    for c in range(grad.shape[0]):
        for x in range(grad.shape[1]):
            solved[c, x] = along * grad[c, x] - across * turned[c, x]
            left[c, x] = observed[c, x] - along * imaged[c, x] + across * second[c, x]
    for copy in copies:
        copy.wait_send()


def finish(*fields):
    wins, sectors = lax.axis_size("win") - 1, lax.axis_size("sector") - 1
    vmem = pl.BlockSpec(memory_space=pltpu.VMEM)
    result = jax.ShapeDtypeStruct(fields[0].shape, jnp.float32)
    return pl.pallas_call(
        finish_kernel,
        out_shape=(result, result),
        in_specs=[vmem] * len(fields),
        out_specs=(vmem, vmem),
        scratch_shapes=[
            pltpu.VMEM((2, 8, 128), jnp.float32),
            pltpu.VMEM((wins, 8, 128), jnp.float32),
            pltpu.VMEM((sectors, 8, 128), jnp.float32),
            pltpu.SemaphoreType.DMA((wins + sectors,)),
            pltpu.SemaphoreType.DMA((wins + sectors,)),
        ],
        compiler_params=pltpu.CompilerParams(
            collective_id=1, has_side_effects=True, vmem_limit_bytes=32 * 1024 * 1024
        ),
    )(*fields)


def fold_kernel(spread, grad, ext, win_in, sec_in, mid, send_sem, recv_sem):
    comps, core_x, core_y = grad.shape[:3]
    rim = KL // 2
    rows = (pl.ds(0, rim), pl.ds(rim, core_x), pl.ds(rim + core_x, rim))
    cols = (pl.ds(0, rim), pl.ds(rim, core_y), pl.ds(rim + core_y, rim))
    place = {axis: lax.axis_index(axis) for axis in ("sector", "win")}
    exists = {}
    for axis, me in place.items():
        exists[axis, -1] = me > 0
        exists[axis, 1] = me < lax.axis_size(axis) - 1

    barrier = pltpu.get_barrier_semaphore()
    for (axis, way), there in exists.items():

        @pl.when(there)
        def _():
            pl.semaphore_signal(
                barrier, inc=1, device_id={axis: place[axis] + way}, device_id_type=MESH
            )

    pl.semaphore_wait(barrier, sum(there.astype(jnp.int32) for there in exists.values()))

    started = []
    slots = {}

    def copy_of(key, axis, way, src, dst):
        slot = slots.setdefault(key, len(slots))
        return link(src, dst, send_sem.at[slot], recv_sem.at[slot], axis, place[axis] + way)

    def send(key, axis, way, src, dst):
        @pl.when(exists[axis, way])
        def _():
            copy_of(key, axis, way, src, dst).start()

        started.append((key, axis, way, src, dst))

    def receive(key, axis, way, src, dst, then=None):
        @pl.when(exists[axis, -way])
        def _():
            copy_of(key, axis, way, src, dst).wait_recv()
            if then is not None:
                then()

    ways = ((0, -1), (1, 1))

    def rim_of(c, part, side):
        return (
            spread.at[c, rows[part], cols[2 * side]],
            win_in.at[side, c, rows[part]],
        )

    pieces = [(c, part) for c in range(comps) for part in (0, 2)] + [(c, 1) for c in range(comps)]
    for c, part in pieces:
            for side, way in ways:
                send(("rim", c, part, side), "win", way, *rim_of(c, part, side))
    def gather_rims(c, part):
        mid[c, rows[part]] = spread[c, rows[part], cols[1]]
        for side, way in ways:

            def add():
                mid[c, rows[part]] += win_in[side, c, rows[part]]

            receive(("rim", c, part, side), "win", way, *rim_of(c, part, side), add)

    for c in range(comps):
        for part in (0, 2):
            gather_rims(c, part)
            side = part // 2
            send(("edge", c, side), "sector", ways[side][1], mid.at[c, rows[part]], sec_in.at[side, c])

    def around(c, side):
        return ext.at[c, rows[1], cols[1]], ext.at[c, rows[2 - 2 * side], cols[1]]

    def beside(c, part, side):
        return ext.at[c, rows[part], cols[1]], ext.at[c, rows[part], cols[2 - 2 * side]]

    for c in range(comps):
        gather_rims(c, 1)
        grad[c] = mid[c, rows[1]]
        for side, way in ways:

            def add_edge():
                grad[c] += sec_in[side, c]

            receive(
                ("edge", c, side), "sector", way, mid.at[c, rows[2 * side]], sec_in.at[side, c], add_edge
            )
        ext[c, rows[1], cols[1]] = grad[c]
        for side, way in ways:
            send(("around", c, side), "sector", way, *around(c, side))
        for side, way in ways:
            send(("beside", c, 1, side), "win", way, *beside(c, 1, side))

    for c in range(comps):
        for side, way in ways:
            part = 2 - 2 * side

            def pass_on():
                for side_y, way_y in ways:

                    @pl.when(exists["win", way_y])
                    def _():
                        copy_of(
                            ("beside", c, part, side_y), "win", way_y, *beside(c, part, side_y)
                        ).start()

            receive(("around", c, side), "sector", way, *around(c, side), pass_on)

            @pl.when(jnp.logical_not(exists["sector", -way]))
            def _():
                ext[c, rows[part]] = jnp.zeros((rim,) + ext.shape[2:], jnp.float32)

        for side, way in ways:
            missing = jnp.logical_not(exists["win", -way])

            @pl.when(missing)
            def _():
                for part, height in ((0, rim), (1, core_x), (2, rim)):
                    ext[c, rows[part], cols[2 - 2 * side]] = jnp.zeros(
                        (height, rim, ext.shape[3]), jnp.float32
                    )

    for c in range(comps):
        for side, way in ways:
            receive(("beside", c, 1, side), "win", way, *beside(c, 1, side))
        for side_x, way_x in ways:
            part = 2 - 2 * side_x

            @pl.when(exists["sector", -way_x])
            def _():
                for side, way in ways:
                    receive(("beside", c, part, side), "win", way, *beside(c, part, side))

                    @pl.when(exists["win", way])
                    def _():
                        copy_of(
                            ("beside", c, part, side), "win", way, *beside(c, part, side)
                        ).wait_send()

    for key, axis, way, src, dst in started:

        @pl.when(exists[axis, way])
        def _():
            copy_of(key, axis, way, src, dst).wait_send()


def fold_and_extend(spread, core_x, core_y):
    comps, wide_x, wide_y, depth = spread.shape
    rim = KL // 2
    count = comps * (6 + 2 + 2 + 6)
    vmem = pl.BlockSpec(memory_space=pltpu.VMEM)
    return pl.pallas_call(
        fold_kernel,
        out_shape=(
            jax.ShapeDtypeStruct((comps, core_x, core_y, depth), jnp.float32),
            jax.ShapeDtypeStruct(spread.shape, jnp.float32),
        ),
        in_specs=[vmem],
        out_specs=(vmem, vmem),
        scratch_shapes=[
            pltpu.VMEM((2, comps, wide_x, rim, depth), jnp.float32),
            pltpu.VMEM((2, comps, rim, core_y, depth), jnp.float32),
            pltpu.VMEM((comps, wide_x, core_y, depth), jnp.float32),
            pltpu.SemaphoreType.DMA((count,)),
            pltpu.SemaphoreType.DMA((count,)),
        ],
        compiler_params=pltpu.CompilerParams(
            collective_id=2, has_side_effects=True, vmem_limit_bytes=40 * 1024 * 1024
        ),
    )(spread)


def index_angles(row_count, col_count, length, offset):
    row_index = (np.arange(row_count, dtype=np.int64)[:, None] + offset) % length
    col_index = np.arange(col_count, dtype=np.int64)[None, :]
    phase = row_index * col_index % length
    angle = phase * (2.0 * math.pi / length)
    return (np.cos(angle).astype(np.float32), np.sin(angle).astype(np.float32))


def half_forward(row_count, length):
    cos_part, sin_part = index_angles(row_count, length // 2 + 1, length, 0)
    return np.stack([cos_part, -sin_part], axis=1)


def full_forward(row_count, length, offset):
    cos_part, sin_part = index_angles(row_count, length, length, offset)
    real_rows = np.stack([cos_part, -sin_part], axis=1)
    imag_rows = np.stack([sin_part, cos_part], axis=1)
    return np.stack([real_rows, imag_rows], axis=0)


def full_inverse(length, out_count):
    cos_part, sin_part = index_angles(length, out_count, length, 0)
    real_rows = np.stack([cos_part, sin_part], axis=1)
    imag_rows = np.stack([-sin_part, cos_part], axis=1)
    return np.stack([real_rows, imag_rows], axis=0)


def half_inverse(length, out_count):
    half_count = length // 2 + 1
    cos_part, sin_part = index_angles(half_count, out_count, length, 0)
    frequency = np.arange(half_count, dtype=np.int64)
    edge = (frequency == 0) | (frequency == length // 2)
    weights = np.where(edge, 1.0, 2.0).astype(np.float32)[:, None]
    return np.stack([cos_part * weights, -sin_part * weights], axis=0)


def spectrum_of(values_in, width_x, width_y, length_z, depth_offset):
    rows_x, rows_y, depth = (values_in.shape[1], values_in.shape[2], values_in.shape[3])
    along_x = jnp.einsum(
        "xrj,mxyz->rjmyz", half_forward(rows_x, width_x), values_in, precision=highest
    )
    along_y = jnp.einsum(
        "rysj,rxmyz->sjxmz", full_forward(rows_y, width_y, 0), along_x, precision=highest
    )
    return jnp.einsum(
        "ryxmz,rzsk->yxmsk", along_y, full_forward(depth, length_z, depth_offset), precision=highest
    )


def values_of(spectrum, out_x, out_y, out_z, width_x, length_z):
    width_y = spectrum.shape[0]
    depth_back = jnp.einsum(
        "yxmsk,skrz->yxmrz", spectrum, full_inverse(length_z, out_z), precision=highest
    )
    table_y = full_inverse(width_y, out_y).transpose(1, 0, 2, 3)
    lateral_y = jnp.einsum("arsy,axmrz->syxmz", table_y, depth_back, precision=highest)
    table_x = half_inverse(width_x, out_x) / np.float32(width_x * width_y * length_z)
    lateral_x = jnp.einsum(
        "sjx,syjmz->mxyz", table_x, lateral_y, precision=highest
    )
    return lateral_x


def kernel_spectrum(flat_kernel, width_x, width_y, length_z):
    kernel = flat_kernel.reshape(4, KD, KL, KL).transpose(0, 2, 3, 1)
    spectrum = spectrum_of(kernel, width_x, width_y, length_z, -(KD // 2))
    return spectrum.reshape(spectrum.shape[0], spectrum.shape[1], 2, 2, 2, spectrum.shape[4])


def correlate(kernel_spec, spectrum):
    kernel_real, kernel_imag = (kernel_spec[..., 0, :], kernel_spec[..., 1, :])
    field_real = spectrum[:, :, None, :, 0, :]
    field_imag = spectrum[:, :, None, :, 1, :]
    real_part = jnp.sum(kernel_real * field_real + kernel_imag * field_imag, axis=3)
    imag_part = jnp.sum(kernel_real * field_imag - kernel_imag * field_real, axis=3)
    return jnp.stack([real_part, imag_part], axis=3)


def convolve(kernel_spec, spectrum):
    kernel_real, kernel_imag = (kernel_spec[..., 0, :], kernel_spec[..., 1, :])
    field_real = spectrum[:, :, :, None, 0, :]
    field_imag = spectrum[:, :, :, None, 1, :]
    real_part = jnp.sum(kernel_real * field_real - kernel_imag * field_imag, axis=2)
    imag_part = jnp.sum(kernel_real * field_imag + kernel_imag * field_real, axis=2)
    return jnp.stack([real_part, imag_part], axis=3)


def hessian_image(extended, kernel_spec, core_x, core_y, length_z):
    width_x, width_y = (extended.shape[1], extended.shape[2])
    spectrum = spectrum_of(extended, width_x, width_y, length_z, 0)
    return values_of(
        correlate(kernel_spec, spectrum), core_x, core_y, extended.shape[3], width_x, length_z
    )


def adjoint_image(values_in, kernel_spec, length_z):
    rows_x, rows_y, depth = (values_in.shape[1], values_in.shape[2], values_in.shape[3])
    width_x, width_y = (rows_x + KL, rows_y + KL)
    spectrum = spectrum_of(values_in, width_x, width_y, length_z, 0)
    spread = values_of(convolve(kernel_spec, spectrum), width_x, width_y, depth, width_x, length_z)
    return fold_and_extend(spread, rows_x, rows_y)


def per_device(observed, psf_bank, psf_ids, weight_ids, list_counts):
    shard_rows = psf_bank.shape[0]
    tiles = psf_bank.reshape(shard_rows, 4 * KD, KL * KL)
    blended = blend(psf_ids, weight_ids, list_counts, tiles)
    core_x, core_y = observed.shape[1:3]
    length_z = observed.shape[3] + KD
    kernel_spec = kernel_spectrum(blended, core_x + KL, core_y + KL, length_z)
    gradient, around = adjoint_image(observed, kernel_spec, length_z)
    imaged = hessian_image(around, kernel_spec, core_x, core_y, length_z)
    turned, around = adjoint_image(imaged, kernel_spec, length_z)
    turned_image = hessian_image(around, kernel_spec, core_x, core_y, length_z)
    return finish(gradient, turned, observed, imaged, turned_image)


def solution(mesh):
    placed = (
        P(None, "sector", "win", None),
        P("sector", None, None, None, None),
        P(None, "win", None),
        P(None, "win", None),
        P(None, "win"),
    )
    return jax.shard_map(
        per_device,
        mesh=mesh,
        in_specs=placed,
        out_specs=(P(None, "sector", "win", None), P(None, "sector", "win", None)),
        check_vma=False,
    )
```

```python
import functools
import math

import jax
import jax.numpy as jnp
import numpy as np
from jax import lax
from jax.experimental import pallas as pl
from jax.experimental.pallas import tpu as pltpu
from jax.sharding import PartitionSpec as P

KL = 32
KD = 16
NW = 16


highest = lax.Precision.HIGH
MESH = pl.DeviceIdType.MESH


def link(src, dst, send_sem, recv_sem, axis, target):
    return pltpu.make_async_remote_copy(
        src_ref=src,
        dst_ref=dst,
        send_sem=send_sem,
        recv_sem=recv_sem,
        device_id={axis: target},
        device_id_type=MESH,
    )


def greet_all(axes):
    barrier = pltpu.get_barrier_semaphore()
    total = 0
    for axis in axes:
        count = lax.axis_size(axis)
        me = lax.axis_index(axis)
        for step in range(1, count):
            pl.semaphore_signal(
                barrier, inc=1, device_id={axis: lax.rem(me + step, count)}, device_id_type=MESH
            )
        total += count - 1
    return lambda: pl.semaphore_wait(barrier, total)


def blend_kernel(ids, levels, counts, bank, out, parts, arrived, send_sem, recv_sem):
    count = lax.axis_size("sector")
    me = lax.axis_index("sector")
    wait_for_all = greet_all(("sector",))

    def factor(window, tile):
        total = jnp.float32(0.0)
        for entry in range(ids.shape[2]):
            named = ids[window, 0, entry] == me * bank.shape[0] + tile
            live = jnp.logical_and(named, entry < counts[window, 0])
            level = (levels[window, 0, entry].astype(jnp.float32) + 1.0) * (1.0 / NW)
            total = total + jnp.where(live, level, 0.0)
        return total

    def partial_sum(window):
        total = factor(window, 0) * bank[0]
        for tile in range(1, bank.shape[0]):
            total = total + factor(window, tile) * bank[tile]
        return total

    copies = []
    for step in range(1, count):
        target = lax.rem(me + step, count)
        parts[step - 1] = partial_sum(target)
        if step == 1:
            wait_for_all()
        copy = link(
            parts.at[step - 1],
            arrived.at[step - 1],
            send_sem.at[step - 1],
            recv_sem.at[step - 1],
            "sector",
            target,
        )
        copy.start()
        copies.append(copy)
    out[...] = partial_sum(me)
    for step, copy in enumerate(copies):
        copy.wait_recv()
        out[...] += arrived[step]
    for copy in copies:
        copy.wait_send()


def blend(ids, levels, counts, bank):
    rows, width = bank.shape[1:]
    others = lax.axis_size("sector") - 1
    slots = pltpu.VMEM((others, rows, width), jnp.float32)
    return pl.pallas_call(
        blend_kernel,
        out_shape=jax.ShapeDtypeStruct((rows, width), jnp.float32),
        in_specs=[
            pl.BlockSpec(memory_space=pltpu.SMEM),
            pl.BlockSpec(memory_space=pltpu.SMEM),
            pl.BlockSpec(memory_space=pltpu.SMEM),
            pl.BlockSpec(memory_space=pltpu.VMEM),
        ],
        out_specs=pl.BlockSpec(memory_space=pltpu.VMEM),
        scratch_shapes=[
            slots,
            slots,
            pltpu.SemaphoreType.DMA((others,)),
            pltpu.SemaphoreType.DMA((others,)),
        ],
        compiler_params=pltpu.CompilerParams(
            collective_id=0, has_side_effects=True, vmem_limit_bytes=32 * 1024 * 1024
        ),
    )(ids, levels, counts, bank)


def finish_kernel(
    grad, turned, observed, imaged, second, solved, left, held, from_win, from_sector, send_sem, recv_sem
):
    pairs = (
        (grad, grad),
        (imaged, imaged),
        (grad, turned),
        (turned, turned),
        (imaged, second),
        (second, second),
    )
    wait_for_all = greet_all(("win", "sector"))
    held[0] = jnp.zeros(held.shape[1:], jnp.float32)
    for row, (one, other) in enumerate(pairs):
        lanes = jnp.sum(one[...] * other[...], axis=(0, 1))
        held[0, row : row + 1] = jnp.sum(lanes, axis=0, keepdims=True)
    wait_for_all()
    base = 0
    copies = []
    for phase, (axis, landing) in enumerate((("win", from_win), ("sector", from_sector))):
        count = lax.axis_size(axis)
        me = lax.axis_index(axis)
        current = []
        for step in range(1, count):
            slot = base + step - 1
            copy = link(
                held.at[phase],
                landing.at[step - 1],
                send_sem.at[slot],
                recv_sem.at[slot],
                axis,
                lax.rem(me + step, count),
            )
            copy.start()
            current.append(copy)
        base += count - 1
        for copy in current:
            copy.wait_recv()
        total = held[phase]
        for step in range(count - 1):
            total = total + landing[step]
        if phase == 0:
            held[1] = total
        copies += current
    sums = [jnp.sum(total[row : row + 1], axis=1, keepdims=True) for row in range(len(pairs))]
    gamma, energy, cross, curve, mixed, last = sums
    step = gamma / energy
    gamma_next = gamma - 2.0 * step * cross + step * step * curve
    keep = 1.0 + gamma_next / gamma
    next_energy = keep * keep * energy - 2.0 * keep * step * mixed + step * step * last
    next_step = gamma_next / next_energy
    along = step + next_step * keep
    across = next_step * step
    for c in range(grad.shape[0]):
        for x in range(grad.shape[1]):
            solved[c, x] = along * grad[c, x] - across * turned[c, x]
            left[c, x] = observed[c, x] - along * imaged[c, x] + across * second[c, x]
    for copy in copies:
        copy.wait_send()


def finish(*fields):
    wins, sectors = lax.axis_size("win") - 1, lax.axis_size("sector") - 1
    vmem = pl.BlockSpec(memory_space=pltpu.VMEM)
    result = jax.ShapeDtypeStruct(fields[0].shape, jnp.float32)
    return pl.pallas_call(
        finish_kernel,
        out_shape=(result, result),
        in_specs=[vmem] * len(fields),
        out_specs=(vmem, vmem),
        scratch_shapes=[
            pltpu.VMEM((2, 8, 128), jnp.float32),
            pltpu.VMEM((wins, 8, 128), jnp.float32),
            pltpu.VMEM((sectors, 8, 128), jnp.float32),
            pltpu.SemaphoreType.DMA((wins + sectors,)),
            pltpu.SemaphoreType.DMA((wins + sectors,)),
        ],
        compiler_params=pltpu.CompilerParams(
            collective_id=1, has_side_effects=True, vmem_limit_bytes=32 * 1024 * 1024
        ),
    )(*fields)


def fold_kernel(spread, grad, ext, win_in, sec_in, mid, send_sem, recv_sem):
    comps, core_x, core_y = grad.shape[:3]
    rim = KL // 2
    rows = (pl.ds(0, rim), pl.ds(rim, core_x), pl.ds(rim + core_x, rim))
    cols = (pl.ds(0, rim), pl.ds(rim, core_y), pl.ds(rim + core_y, rim))
    place = {axis: lax.axis_index(axis) for axis in ("sector", "win")}
    exists = {}
    for axis, me in place.items():
        exists[axis, -1] = me > 0
        exists[axis, 1] = me < lax.axis_size(axis) - 1

    barrier = pltpu.get_barrier_semaphore()
    for (axis, way), there in exists.items():

        @pl.when(there)
        def _():
            pl.semaphore_signal(
                barrier, inc=1, device_id={axis: place[axis] + way}, device_id_type=MESH
            )

    pl.semaphore_wait(barrier, sum(there.astype(jnp.int32) for there in exists.values()))

    started = []
    slots = {}

    def copy_of(key, axis, way, src, dst):
        slot = slots.setdefault(key, len(slots))
        return link(src, dst, send_sem.at[slot], recv_sem.at[slot], axis, place[axis] + way)

    def send(key, axis, way, src, dst):
        @pl.when(exists[axis, way])
        def _():
            copy_of(key, axis, way, src, dst).start()

        started.append((key, axis, way, src, dst))

    def receive(key, axis, way, src, dst, then=None):
        @pl.when(exists[axis, -way])
        def _():
            copy_of(key, axis, way, src, dst).wait_recv()
            if then is not None:
                then()

    ways = ((0, -1), (1, 1))

    def rim_of(c, part, side):
        return (
            spread.at[c, rows[part], cols[2 * side]],
            win_in.at[side, c, rows[part]],
        )

    pieces = [(c, part) for c in range(comps) for part in (0, 2)] + [(c, 1) for c in range(comps)]
    for c, part in pieces:
            for side, way in ways:
                send(("rim", c, part, side), "win", way, *rim_of(c, part, side))
    def gather_rims(c, part):
        mid[c, rows[part]] = spread[c, rows[part], cols[1]]
        for side, way in ways:

            def add():
                mid[c, rows[part]] += win_in[side, c, rows[part]]

            receive(("rim", c, part, side), "win", way, *rim_of(c, part, side), add)

    for c in range(comps):
        for part in (0, 2):
            gather_rims(c, part)
            side = part // 2
            send(("edge", c, side), "sector", ways[side][1], mid.at[c, rows[part]], sec_in.at[side, c])

    def around(c, side):
        return ext.at[c, rows[1], cols[1]], ext.at[c, rows[2 - 2 * side], cols[1]]

    def beside(c, part, side):
        return ext.at[c, rows[part], cols[1]], ext.at[c, rows[part], cols[2 - 2 * side]]

    for c in range(comps):
        gather_rims(c, 1)
        grad[c] = mid[c, rows[1]]
        for side, way in ways:

            def add_edge():
                grad[c] += sec_in[side, c]

            receive(
                ("edge", c, side), "sector", way, mid.at[c, rows[2 * side]], sec_in.at[side, c], add_edge
            )
        ext[c, rows[1], cols[1]] = grad[c]
        for side, way in ways:
            send(("around", c, side), "sector", way, *around(c, side))
        for side, way in ways:
            send(("beside", c, 1, side), "win", way, *beside(c, 1, side))

    for c in range(comps):
        for side, way in ways:
            part = 2 - 2 * side

            def pass_on():
                for side_y, way_y in ways:

                    @pl.when(exists["win", way_y])
                    def _():
                        copy_of(
                            ("beside", c, part, side_y), "win", way_y, *beside(c, part, side_y)
                        ).start()

            receive(("around", c, side), "sector", way, *around(c, side), pass_on)

            @pl.when(jnp.logical_not(exists["sector", -way]))
            def _():
                ext[c, rows[part]] = jnp.zeros((rim,) + ext.shape[2:], jnp.float32)

        for side, way in ways:
            missing = jnp.logical_not(exists["win", -way])

            @pl.when(missing)
            def _():
                for part, height in ((0, rim), (1, core_x), (2, rim)):
                    ext[c, rows[part], cols[2 - 2 * side]] = jnp.zeros(
                        (height, rim, ext.shape[3]), jnp.float32
                    )

    for c in range(comps):
        for side, way in ways:
            receive(("beside", c, 1, side), "win", way, *beside(c, 1, side))
        for side_x, way_x in ways:
            part = 2 - 2 * side_x

            @pl.when(exists["sector", -way_x])
            def _():
                for side, way in ways:
                    receive(("beside", c, part, side), "win", way, *beside(c, part, side))

                    @pl.when(exists["win", way])
                    def _():
                        copy_of(
                            ("beside", c, part, side), "win", way, *beside(c, part, side)
                        ).wait_send()

    for key, axis, way, src, dst in started:

        @pl.when(exists[axis, way])
        def _():
            copy_of(key, axis, way, src, dst).wait_send()


def fold_and_extend(spread, core_x, core_y):
    comps, wide_x, wide_y, depth = spread.shape
    rim = KL // 2
    count = comps * (6 + 2 + 2 + 6)
    vmem = pl.BlockSpec(memory_space=pltpu.VMEM)
    return pl.pallas_call(
        fold_kernel,
        out_shape=(
            jax.ShapeDtypeStruct((comps, core_x, core_y, depth), jnp.float32),
            jax.ShapeDtypeStruct(spread.shape, jnp.float32),
        ),
        in_specs=[vmem],
        out_specs=(vmem, vmem),
        scratch_shapes=[
            pltpu.VMEM((2, comps, wide_x, rim, depth), jnp.float32),
            pltpu.VMEM((2, comps, rim, core_y, depth), jnp.float32),
            pltpu.VMEM((comps, wide_x, core_y, depth), jnp.float32),
            pltpu.SemaphoreType.DMA((count,)),
            pltpu.SemaphoreType.DMA((count,)),
        ],
        compiler_params=pltpu.CompilerParams(
            collective_id=2, has_side_effects=True, vmem_limit_bytes=40 * 1024 * 1024
        ),
    )(spread)


def index_angles(row_count, col_count, length, offset):
    row_index = (np.arange(row_count, dtype=np.int64)[:, None] + offset) % length
    col_index = np.arange(col_count, dtype=np.int64)[None, :]
    phase = row_index * col_index % length
    angle = phase * (2.0 * math.pi / length)
    return (np.cos(angle).astype(np.float32), np.sin(angle).astype(np.float32))


def half_forward(row_count, length):
    cos_part, sin_part = index_angles(row_count, length // 2 + 1, length, 0)
    return np.stack([cos_part, -sin_part], axis=1)


def full_forward(row_count, length, offset):
    cos_part, sin_part = index_angles(row_count, length, length, offset)
    real_rows = np.stack([cos_part, -sin_part], axis=1)
    imag_rows = np.stack([sin_part, cos_part], axis=1)
    return np.stack([real_rows, imag_rows], axis=0)


def full_inverse(length, out_count):
    cos_part, sin_part = index_angles(length, out_count, length, 0)
    real_rows = np.stack([cos_part, sin_part], axis=1)
    imag_rows = np.stack([-sin_part, cos_part], axis=1)
    return np.stack([real_rows, imag_rows], axis=0)


def half_inverse(length, out_count):
    half_count = length // 2 + 1
    cos_part, sin_part = index_angles(half_count, out_count, length, 0)
    frequency = np.arange(half_count, dtype=np.int64)
    edge = (frequency == 0) | (frequency == length // 2)
    weights = np.where(edge, 1.0, 2.0).astype(np.float32)[:, None]
    return np.stack([cos_part * weights, -sin_part * weights], axis=0)


def spectrum_of(values_in, width_x, width_y, length_z, depth_offset):
    rows_x, rows_y, depth = (values_in.shape[1], values_in.shape[2], values_in.shape[3])
    along_x = jnp.einsum(
        "xrj,mxyz->rjmyz", half_forward(rows_x, width_x), values_in, precision=highest
    )
    along_y = jnp.einsum(
        "rysj,rxmyz->sjxmz", full_forward(rows_y, width_y, 0), along_x, precision=highest
    )
    return jnp.einsum(
        "ryxmz,rzsk->yxmsk", along_y, full_forward(depth, length_z, depth_offset), precision=highest
    )


def values_of(spectrum, out_x, out_y, out_z, width_x, length_z):
    width_y = spectrum.shape[0]
    depth_back = jnp.einsum(
        "yxmsk,skrz->yxmrz", spectrum, full_inverse(length_z, out_z), precision=highest
    )
    table_y = full_inverse(width_y, out_y).transpose(1, 0, 2, 3)
    lateral_y = jnp.einsum("arsy,axmrz->syxmz", table_y, depth_back, precision=highest)
    table_x = half_inverse(width_x, out_x) / np.float32(width_x * width_y * length_z)
    lateral_x = jnp.einsum(
        "sjx,syjmz->mxyz", table_x, lateral_y, precision=highest
    )
    return lateral_x


def kernel_spectrum(flat_kernel, width_x, width_y, length_z):
    kernel = flat_kernel.reshape(4, KD, KL, KL).transpose(0, 2, 3, 1)
    spectrum = spectrum_of(kernel, width_x, width_y, length_z, -(KD // 2))
    return spectrum.reshape(spectrum.shape[0], spectrum.shape[1], 2, 2, 2, spectrum.shape[4])


def correlate(kernel_spec, spectrum):
    kernel_real, kernel_imag = (kernel_spec[..., 0, :], kernel_spec[..., 1, :])
    field_real = spectrum[:, :, None, :, 0, :]
    field_imag = spectrum[:, :, None, :, 1, :]
    real_part = jnp.sum(kernel_real * field_real + kernel_imag * field_imag, axis=3)
    imag_part = jnp.sum(kernel_real * field_imag - kernel_imag * field_real, axis=3)
    return jnp.stack([real_part, imag_part], axis=3)


def convolve(kernel_spec, spectrum):
    kernel_real, kernel_imag = (kernel_spec[..., 0, :], kernel_spec[..., 1, :])
    field_real = spectrum[:, :, :, None, 0, :]
    field_imag = spectrum[:, :, :, None, 1, :]
    real_part = jnp.sum(kernel_real * field_real - kernel_imag * field_imag, axis=2)
    imag_part = jnp.sum(kernel_real * field_imag + kernel_imag * field_real, axis=2)
    return jnp.stack([real_part, imag_part], axis=3)


def hessian_image(extended, kernel_spec, core_x, core_y, length_z):
    width_x, width_y = (extended.shape[1], extended.shape[2])
    spectrum = spectrum_of(extended, width_x, width_y, length_z, 0)
    return values_of(
        correlate(kernel_spec, spectrum), core_x, core_y, extended.shape[3], width_x, length_z
    )


def adjoint_image(values_in, kernel_spec, length_z):
    rows_x, rows_y, depth = (values_in.shape[1], values_in.shape[2], values_in.shape[3])
    width_x, width_y = (rows_x + KL, rows_y + KL)
    spectrum = spectrum_of(values_in, width_x, width_y, length_z, 0)
    spread = values_of(convolve(kernel_spec, spectrum), width_x, width_y, depth, width_x, length_z)
    return fold_and_extend(spread, rows_x, rows_y)


def per_device(observed, psf_bank, psf_ids, weight_ids, list_counts):
    shard_rows = psf_bank.shape[0]
    tiles = psf_bank.reshape(shard_rows, 4 * KD, KL * KL)
    blended = blend(psf_ids, weight_ids, list_counts, tiles)
    core_x, core_y = observed.shape[1:3]
    length_z = observed.shape[3] + KD
    kernel_spec = kernel_spectrum(blended, core_x + KL, core_y + KL, length_z)
    gradient, around = adjoint_image(observed, kernel_spec, length_z)
    imaged = hessian_image(around, kernel_spec, core_x, core_y, length_z)
    turned, around = adjoint_image(imaged, kernel_spec, length_z)
    turned_image = hessian_image(around, kernel_spec, core_x, core_y, length_z)
    return finish(gradient, turned, observed, imaged, turned_image)


def solution(mesh):
    placed = (
        P(None, "sector", "win", None),
        P("sector", None, None, None, None),
        P(None, "win", None),
        P(None, "win", None),
        P(None, "win"),
    )
    return jax.shard_map(
        per_device,
        mesh=mesh,
        in_specs=placed,
        out_specs=(P(None, "sector", "win", None), P(None, "sector", "win", None)),
        check_vma=False,
    )
```
